32 devices in a mesh: inst: 8 (over z, x), tp: 4 (over y, core).
Axes of the slice: x: 2, y: 2, z: 4, core: 2. Of those that a mesh axis runs over, the one named last changes fastest.
Arguments:
- queries: bfloat16 [2, 256, 1024], P(None, 'inst', 'tp'), may hold values from -120 to 120
- stored_keys: bfloat16 [256, 128, 512], P('inst', None, 'tp'), may hold values from -6.1 to 6.1, as said below
- stored_values: bfloat16 [256, 128, 512], P('inst', None, 'tp'), may hold values from -6 to 6, as said below
- incoming_keys: bfloat16 [2, 256, 512], P(None, 'inst', 'tp'), may hold values from -6 to 6, as said below
- incoming_values: bfloat16 [2, 256, 512], P(None, 'inst', 'tp'), may hold values from -6 to 6, as said below
- cache_length_rows: int32 [256], P('inst'), may hold values from 2 to 128
- output_matrix: bfloat16 [1024, 4096], P('tp'), may hold values from -0.25 to 0.25
- adapter_down_weight: bfloat16 [32, 1024, 64], P('inst', 'tp'), may hold values from -0.1875 to 0.1875
- adapter_up_weight: bfloat16 [32, 64, 4096], P('inst', None, 'tp'), may hold values from -0.75 to 0.75
- host: int32 [256, 1], P('inst'), may hold values from 0 to 7; in each aligned block of 32 rows (0 to 31, 32 to 63, ...) at most 8 rows name the same one
- slot: int32 [256], P('inst'), may hold values from 0 to 3
Outputs:
- projected: bfloat16 [2, 256, 4096], P(None, 'inst', 'tp')
The draws below stay inside these ranges and needn't reach their ends.
Inputs may be any that keep to these rules, and one draw needn't show every extreme that they name: In each instance's rows at most 8 rows name one host, a bound that some block reaches. `stored_keys`: copies c and c' of a head are equal where c // 4 == c' // 4. `incoming_keys`: copies equal as in stored_keys. `stored_values`: copies equal as in stored_keys. `incoming_values`: copies equal as in stored_keys.
All inputs are finite; a program needn't handle non-finite values.
Results may differ from the reference program's by a relative error of at most 0.02.
Values may be sent and summed in bfloat16 or wider, within the bound.
A program may use at most 64 MiB of HBM per device.

```python
import math
import jax
import jax.numpy as jnp
import numpy as np
from jax import lax

OUTPUT_FEATURES = 4096
HEAD_SIZE = 128
QH_DEV = 2
ADAPTER_RANK = 64
STEPS = 2
ROWS = 32
CTX = 128
ADP_DEV = 4
QUERY_HEAD_COUNT = 8
KV_HEADS = 1
TOKENS = 256
ADAPTER_TOTAL = 32
CAP = 8
N_INST = 8
N_TP = 4


def expand_heads(field):
    lead = field.shape[:-2]
    repeated = jnp.repeat(field, N_TP // KV_HEADS, axis=-2)
    return repeated.reshape(lead + (N_TP * HEAD_SIZE,))


def shared_keys(key):
    cached = jax.random.truncated_normal(jax.random.fold_in(key, 101), -6.0, 6.0, (TOKENS, CTX, KV_HEADS, HEAD_SIZE), jnp.float32)
    fresh = jax.random.truncated_normal(jax.random.fold_in(key, 102), -6.0, 6.0, (STEPS, TOKENS, KV_HEADS, HEAD_SIZE), jnp.float32)
    return (expand_heads(cached), expand_heads(fresh))


def draw_stored_keys(key, part):
    cached, fresh = shared_keys(key)
    return cached.astype(jnp.bfloat16)


def draw_incoming_keys(key, part):
    cached, fresh = shared_keys(key)
    return fresh.astype(jnp.bfloat16)


def draw_queries(key, part):
    key = jax.random.fold_in(key, 3)
    drawn = jax.random.truncated_normal(key, -6.0, 6.0, (STEPS, TOKENS, QUERY_HEAD_COUNT * HEAD_SIZE), jnp.float32)
    return drawn.astype(jnp.bfloat16)


def draw_stored_values(key, part):
    key = jax.random.fold_in(key, 4)
    values = jax.random.truncated_normal(key, -6.0, 6.0, (TOKENS, CTX, KV_HEADS, HEAD_SIZE), jnp.float32)
    return expand_heads(values).astype(jnp.bfloat16)


def draw_incoming_values(key, part):
    key = jax.random.fold_in(key, 5)
    values = jax.random.truncated_normal(key, -6.0, 6.0, (STEPS, TOKENS, KV_HEADS, HEAD_SIZE), jnp.float32)
    return expand_heads(values).astype(jnp.bfloat16)


def with_ends(drawn, key, low, top_value):
    dims = drawn.shape
    index_at = [jax.random.randint(jax.random.fold_in(key, axis), (), 0, dims[axis]) for axis in range(len(dims))]
    drawn = drawn.at[tuple(index_at)].set(low)
    longest = dims.index(max(dims))
    index_at[longest] = (index_at[longest] + 1) % dims[longest]
    return drawn.at[tuple(index_at)].set(top_value)


def strengthened(entries, key, source, target, parts, factor):
    owner, partner = [(jnp.arange(entries.shape[axis_at]) // (entries.shape[axis_at] // parts)).reshape([-1 if axis == axis_at else 1 for axis in range(entries.ndim)]) for axis_at in (source, target)]
    chosen = jax.random.permutation(key, parts)[partner]
    strong = (owner == chosen) | (owner == (partner + parts // 2) % parts)
    return jnp.where(strong, factor * entries, entries)


def block_levels(rng, dims, cuts, smallest, high):
    def one(axis_at, shards_of):
        draws = jax.random.uniform(jax.random.fold_in(jax.random.fold_in(rng, 6), axis_at), (shards_of,), jnp.float32, smallest / len(cuts), high / len(cuts))
        return jnp.repeat(jnp.exp(draws), dims[axis_at] // shards_of).reshape((-1,) + (1,) * (len(dims) - axis_at - 1))

    factor_of = one(*cuts[0])
    for cut in cuts[1:]:
        factor_of = factor_of * one(*cut)
    return factor_of


def assign_block(rng, own, number, rows, number_of, top, reach, lean):
    ranking = jax.random.permutation(rng, number_of)
    packed, ordinary = load_shares(number_of, rows * top, reach, lean, True), load_shares(number_of, rows * top, reach, lean, False)
    places = jnp.arange(number_of)

    def named(sizes, turn):
        used = int((sizes > 0).sum())
        fixed = max(1, used // 4)
        passed = fixed + (places - fixed + turn * (used - fixed)) % max(1, number_of - fixed)
        return jnp.zeros((number_of,), jnp.int32).at[ranking[jnp.where(places < fixed, places, passed)]].set(jnp.asarray(sizes, jnp.int32))

    sizes = jnp.where(number % 4 == 0, named(packed, number // 4), named(ordinary, number - number // 4 - 1))
    mixed = jax.random.permutation(jax.random.fold_in(own, 3), number_of)
    donor, sink = mixed[0:number_of // 2 * 2:2], mixed[1:number_of // 2 * 2:2]
    slack = jnp.minimum(sizes[donor] - 1, reach - sizes[sink]) // 2
    slack = jnp.where((donor == ranking[0]) | (sink == ranking[0]) | (sizes[sink] == 0), 0, jnp.maximum(slack, 0))
    passed = jax.random.randint(jax.random.fold_in(own, 4), (number_of // 2,), 0, 1 << 20) % (slack + 1)
    sizes = sizes.at[donor].add(-passed).at[sink].add(passed)
    members = jnp.searchsorted(jnp.cumsum(sizes), jnp.arange(rows * top), side="right").astype(jnp.int32)
    table = members.reshape(top, rows).T
    table = table[jax.random.permutation(jax.random.fold_in(own, 1), rows)]
    turn = jax.random.randint(jax.random.fold_in(own, 2), (rows, 1), 0, top)
    return jnp.take_along_axis(table, (jnp.arange(top)[None, :] + turn) % top, axis=1)


def load_shares(number_of, total, reach, slope, full):
    portions = [(1 << 20) // math.isqrt(grade ** slope) + 1 for grade in range(1, number_of + 1)]
    largest = reach if full else min(reach, max(-(-total // number_of), total * portions[0] // sum(portions)))
    least = 1 if total - largest >= number_of - 1 else 0
    counts, rest = [largest] + [least] * (number_of - 1), total - largest - least * (number_of - 1)
    while rest > 0:
        movable = [i for i in range(1, number_of) if counts[i] < largest] or [i for i in range(1, number_of) if counts[i] < reach]
        pool, remaining = sum([portions[i] for i in movable]), rest
        for i in movable:
            extra = min(reach - counts[i], max(1, remaining * portions[i] // pool), rest)
            counts[i] = counts[i] + extra
            rest = rest - extra
    return np.array(counts)


def noise(stream_key, shape, deviation, limit, pieces=(), kind=jnp.bfloat16):
    gain = block_levels(stream_key, shape, pieces, -0.22, 0.18) if pieces else 1.0
    values = jax.random.normal(stream_key, shape, jnp.float32) * deviation * gain
    return jnp.minimum(jnp.maximum(values, -limit), limit).astype(kind)


def bell_draw_with(rng, dims, spread, limit, split, heavy, held_as=jnp.bfloat16):
    array = spread * jax.random.normal(rng, dims, jnp.float32)
    if split:
        array = array * block_levels(rng, dims, split, -0.22, 0.18)
    return jnp.clip(strengthened(array, jax.random.fold_in(rng, 3), *heavy), -limit, limit).astype(held_as)


def setup_inputs(seed: int = 0) -> dict:
    keys = jax.random.split(jax.random.key(seed), 12)
    queries = draw_queries(jax.random.fold_in(keys[11], 71), 0)
    stored_keys = draw_stored_keys(jax.random.fold_in(keys[11], 71), 0)
    stored_values = draw_stored_values(jax.random.fold_in(keys[11], 71), 0)
    incoming_keys = draw_incoming_keys(jax.random.fold_in(keys[11], 71), 0)
    incoming_values = draw_incoming_values(jax.random.fold_in(keys[11], 71), 0)
    cache_length_rows = with_ends(jax.random.randint(keys[5], (TOKENS,), 2, CTX + 1), jax.random.fold_in(keys[5], 1), 2, CTX).astype(jnp.int32)
    output_matrix = bell_draw_with(keys[6], (QUERY_HEAD_COUNT * HEAD_SIZE, OUTPUT_FEATURES), (QUERY_HEAD_COUNT * HEAD_SIZE) ** -0.5, 0.25, ((0, 4),), (0, 1, 4, 2.0))
    adapter_down_weight = noise(keys[7], (ADAPTER_TOTAL, QUERY_HEAD_COUNT * HEAD_SIZE, ADAPTER_RANK), (QUERY_HEAD_COUNT * HEAD_SIZE) ** -0.5, 0.1875, ((0, 8), (1, 4)))
    adapter_up_weight = noise(keys[8], (ADAPTER_TOTAL, ADAPTER_RANK, OUTPUT_FEATURES), ADAPTER_RANK ** -0.5, 0.75, ((0, 8), (2, 4)))
    host_keys = jax.random.split(jax.random.fold_in(keys[9], 1), TOKENS // ROWS)
    host_turns = jax.random.permutation(jax.random.fold_in(keys[9], 3), TOKENS // ROWS)
    host = jax.vmap(lambda own, number: assign_block(jax.random.fold_in(keys[9], 2), own, number, ROWS, N_INST, 1, CAP, 2))(host_keys, host_turns).reshape((TOKENS, 1))
    slot = with_ends(jax.random.randint(keys[10], (TOKENS,), 0, ADP_DEV), jax.random.fold_in(keys[10], 1), 0, ADP_DEV - 1).astype(jnp.int32)
    return {"queries": queries, "stored_keys": stored_keys, "stored_values": stored_values, "incoming_keys": incoming_keys, "incoming_values": incoming_values, "cache_length_rows": cache_length_rows, "output_matrix": output_matrix, "adapter_down_weight": adapter_down_weight, "adapter_up_weight": adapter_up_weight, "host": host, "slot": slot}


def attend_block(query_block, cached_keys, cached_values, fresh_keys, fresh_values, lengths):
    row_count = cached_keys.shape[0]
    copies = N_TP
    score_scale = 1.0 / math.sqrt(HEAD_SIZE)
    keys_view = cached_keys.reshape(row_count, CTX, copies, HEAD_SIZE).astype(jnp.float32)
    values_view = cached_values.reshape(row_count, CTX, copies, HEAD_SIZE).astype(jnp.float32)
    fresh_key_view = fresh_keys.reshape(STEPS, row_count, copies, HEAD_SIZE).astype(jnp.float32)
    fresh_value_view = fresh_values.reshape(STEPS, row_count, copies, HEAD_SIZE).astype(jnp.float32)
    visible = jnp.arange(CTX, dtype=jnp.int32)[None, None, None, :] < lengths[:, None, None, None]
    outputs = []
    for step_index in range(STEPS):
        query_heads = query_block[step_index].reshape(row_count, copies, QH_DEV, HEAD_SIZE).astype(jnp.float32)
        scores = jnp.einsum('bgqd,bcgd->bgqc', query_heads, keys_view) * score_scale
        scores = jnp.where(visible, scores, -1e+30)
        fresh_scores = jnp.einsum('bgqd,sbgd->bgqs', query_heads, fresh_key_view[:step_index + 1]) * score_scale
        highest = jnp.maximum(lax.optimization_barrier(jnp.max(scores, axis=-1, keepdims=True)), lax.optimization_barrier(jnp.max(fresh_scores, axis=-1, keepdims=True)))
        cached_exp = jnp.exp(scores - highest)
        fresh_exp = jnp.exp(fresh_scores - highest)
        denominator = lax.optimization_barrier(jnp.sum(cached_exp, axis=-1, keepdims=True)) + lax.optimization_barrier(jnp.sum(fresh_exp, axis=-1, keepdims=True))
        cached_weight = (cached_exp / denominator).astype(jnp.bfloat16)
        fresh_weight = (fresh_exp / denominator).astype(jnp.bfloat16)
        mixed_heads = jnp.einsum('bgqc,bcgd->bgqd', cached_weight.astype(jnp.float32), values_view)
        mixed_heads = mixed_heads + jnp.einsum('bgqs,sbgd->bgqd', fresh_weight.astype(jnp.float32), fresh_value_view[:step_index + 1])
        outputs.append(mixed_heads.astype(jnp.bfloat16).reshape(row_count, QUERY_HEAD_COUNT * HEAD_SIZE))
    return jnp.stack(outputs)

def reference(queries, stored_keys, stored_values, incoming_keys, incoming_values, cache_length_rows, output_matrix, adapter_down_weight, adapter_up_weight, host, slot):
    adapter = (host[:, 0] * ADP_DEV + slot).astype(jnp.int32)
    block_rows = math.gcd(TOKENS, 32)
    blocks = TOKENS // block_rows

    def run_block(block_index):
        first_row = (block_index * block_rows).astype(jnp.int32)
        query_block = lax.dynamic_slice_in_dim(queries, first_row, block_rows, 1)
        cached_keys = lax.dynamic_slice_in_dim(stored_keys, first_row, block_rows, 0)
        cached_values = lax.dynamic_slice_in_dim(stored_values, first_row, block_rows, 0)
        fresh_keys = lax.dynamic_slice_in_dim(incoming_keys, first_row, block_rows, 1)
        fresh_values = lax.dynamic_slice_in_dim(incoming_values, first_row, block_rows, 1)
        lengths = lax.dynamic_slice_in_dim(cache_length_rows, first_row, block_rows, 0)
        adapter_tile_rows = lax.dynamic_slice_in_dim(adapter, first_row, block_rows, 0)
        attention_output = attend_block(query_block, cached_keys, cached_values, fresh_keys, fresh_values, lengths)
        down_weight_rows = adapter_down_weight[adapter_tile_rows].astype(jnp.float32)
        rank_products = jnp.einsum('qnc,ncl->qnl', attention_output.astype(jnp.float32), down_weight_rows).astype(jnp.bfloat16)
        up_weight_rows = adapter_up_weight[adapter_tile_rows].astype(jnp.float32)
        adapter_update = jnp.einsum('ztm,tmh->zth', rank_products.astype(jnp.float32), up_weight_rows)
        return (attention_output, adapter_update)
    attention_output, adapter_update = lax.map(run_block, jnp.arange(blocks, dtype=jnp.int32))
    attention_output = jnp.transpose(attention_output, (1, 0, 2, 3)).reshape(STEPS, TOKENS, QUERY_HEAD_COUNT * HEAD_SIZE)
    adapter_update = jnp.transpose(adapter_update, (1, 0, 2, 3)).reshape(STEPS, TOKENS, OUTPUT_FEATURES)
    base_sum = jnp.dot(attention_output.reshape(STEPS * TOKENS, QUERY_HEAD_COUNT * HEAD_SIZE), output_matrix, preferred_element_type=jnp.float32)
    base_sum = base_sum.reshape(STEPS, TOKENS, OUTPUT_FEATURES)
    return (base_sum + adapter_update).astype(jnp.bfloat16)
```

```python
import functools
import math

import jax
import jax.numpy as jnp
from jax import lax
from jax.experimental import pallas as pl
from jax.experimental.pallas import tpu as pltpu
from jax.sharding import PartitionSpec as P

MESH = pl.DeviceIdType.MESH
BF = jnp.bfloat16
F32 = jnp.float32
TILE = 16
LANES = 128


def log2(n):
    assert n & (n - 1) == 0
    return n.bit_length() - 1


def rows_iota(shape):
    return lax.broadcasted_iota(jnp.int32, shape, 0)


def lanes_iota(shape):
    return lax.broadcasted_iota(jnp.int32, shape, 1)


def dot(a, b):
    return jnp.dot(a, b, preferred_element_type=F32)


def dot_t(a, b):
    return lax.dot_general(a, b, (((1,), (1,)), ((), ())), preferred_element_type=F32)


def one_hot(mask):
    return jnp.where(mask, 1.0, 0.0).astype(BF)


def kernel(
    n_inst, n_tp, cap,
    q_ref, kn_ref, vn_ref, len_ref, host_ref, slot_ref,
    k_hbm, v_hbm, w_hbm, dn_hbm, up_hbm,
    out_ref,
    k_buf, v_buf, w_buf, dn_buf, up_buf, dn_flat,
    meta_s, meta_r, x_s, x_r, dl_s, dl_r, rk_s, rk_r,
    b1_s, b1_r, b2_s, b2_r, own,
    in_sem, meta_ss, meta_rs, x_ss, x_rs, dl_ss, dl_rs, rk_ss, rk_rs,
    b1_ss, b1_rs, b2_ss, b2_rs,
):
    steps, rows, width = q_ref.shape
    head = kn_ref.shape[2]
    heads = width // head
    slots = k_buf.shape[1]
    per_row = steps * heads
    cols = rows * per_row
    pack = meta_s.shape[1]
    total = n_inst * pack
    adapters, _, rank = dn_buf.shape
    chunks = adapters * rank // LANES
    out_cols = up_buf.shape[2]
    n_y = n_tp // 2
    me = lax.axis_index("inst")
    tp = lax.axis_index("tp")
    y = tp // 2
    core = lax.rem(tp, 2)

    def inst_at(k):
        return (lax.rem(me + k + n_inst, n_inst), tp)

    def tp_at(k):
        return (me, lax.rem(tp + k, n_tp))

    def remote(src, dst, send, recv, where):
        return pltpu.make_async_remote_copy(
            src_ref=src, dst_ref=dst, send_sem=send, recv_sem=recv,
            device_id=where, device_id_type=MESH,
        )

    barrier = pltpu.get_barrier_semaphore()
    for k in range(1, n_inst):
        pl.semaphore_signal(barrier, inc=1, device_id=inst_at(k), device_id_type=MESH)
    for k in range(1, n_tp):
        pl.semaphore_signal(barrier, inc=1, device_id=tp_at(k), device_id_type=MESH)
    loads = []
    for at, (src, dst) in enumerate(
        ((k_hbm, k_buf), (v_hbm, v_buf), (w_hbm, w_buf), (dn_hbm, dn_buf), (up_hbm, up_buf))
    ):
        load = pltpu.make_async_copy(src, dst, in_sem.at[at])
        load.start()
        loads.append(load)

    host_lane = host_ref[...].astype(F32)
    slot_lane = slot_ref[...].astype(F32)
    here = me.astype(F32)
    square = (rows, rows)
    ri, li = rows_iota(square), lanes_iota(square)
    host_col = jnp.sum(jnp.where(ri == li, host_lane, 0.0), axis=1, keepdims=True)
    same = jnp.broadcast_to(host_col, square) == jnp.broadcast_to(host_lane, square)
    pos_lane = jnp.sum(jnp.where(same & (ri < li), 1.0, 0.0), axis=0, keepdims=True)
    pos_col = jnp.sum(jnp.where(same & (li < ri), 1.0, 0.0), axis=1, keepdims=True)

    def place(host, pos):
        away = host - here
        away = jnp.where(away < 0.0, away + float(n_inst), away)
        return away * float(pack) + pos

    to_lane = place(host_lane, pos_lane).astype(jnp.int32)
    to_col = place(host_col, pos_col).astype(jnp.int32)
    pack_i = rows_iota((total, rows))
    packs = [pack_i == to_lane + step * cap for step in range(steps)]
    slot_packed = jnp.zeros((total, 1), F32)
    for chosen in packs:
        slot_packed += jnp.sum(jnp.where(chosen, slot_lane, 0.0), axis=1, keepdims=True)
    slot_packed = jnp.broadcast_to(slot_packed, (total, LANES)).astype(BF)
    meta_s[...] = slot_packed.reshape(n_inst, pack, LANES)
    meta_r[0] = slot_packed[:pack]

    pl.semaphore_wait(barrier, n_inst - 1 + n_tp - 1)
    meta_copies = []
    for k in range(1, n_inst):
        copy = remote(meta_s.at[k], meta_r.at[k], meta_ss.at[k], meta_rs.at[k], inst_at(k))
        copy.start()
        meta_copies.append(copy)

    ci = rows_iota((cols, cols))
    cj = lanes_iota((cols, cols))
    into = one_hot(cj == ((ci & (per_row - 1)) << log2(rows)) + (ci >> log2(per_row)))
    back = one_hot(ci == ((cj & (per_row - 1)) << log2(rows)) + (cj >> log2(per_row)))
    q_all = jnp.concatenate(
        [q_ref[s, :, h * head:(h + 1) * head] for s in range(steps) for h in range(heads)], axis=0
    )
    q_lines = dot(into, q_all)
    q_bf = q_lines.astype(BF)
    spread = rows_iota((cols, rows)) >> log2(per_row) == lanes_iota((cols, rows))
    lengths = jnp.sum(
        jnp.where(spread, len_ref[...].astype(F32), 0.0), axis=1, keepdims=True
    ).astype(jnp.int32)
    spread_bf = one_hot(spread)
    scale = 1.0 / math.sqrt(head)
    step_of = (rows_iota((cols, 1)) & (per_row - 1)) >> log2(heads)
    fresh = []
    for s in range(steps):
        value = jnp.sum(q_lines * dot(spread_bf, kn_ref[s]), axis=1, keepdims=True) * scale
        fresh.append(jnp.where(step_of >= s, value, -1e30))
    group = TILE // per_row
    group_of = rows_iota((TILE, slots)) >> log2(per_row)
    loads[0].wait()
    scores = []
    for g in range(rows // group):
        keys = k_buf[g * group:(g + 1) * group].reshape(group * slots, head)
        raw = dot_t(q_bf[g * TILE:(g + 1) * TILE], keys)
        picked = raw[:, :slots]
        for j in range(1, group):
            picked = jnp.where(group_of == j, raw[:, j * slots:(j + 1) * slots], picked)
        scores.append(picked)
    scores = jnp.concatenate(scores, axis=0) * scale
    scores = jnp.where(lanes_iota((cols, slots)) < lengths, scores, -1e30)
    highest = jnp.max(scores, axis=1, keepdims=True)
    for value in fresh:
        highest = jnp.maximum(highest, value)
    cached_exp = jnp.exp(scores - highest)
    fresh_exp = [jnp.exp(value - highest) for value in fresh]
    denominator = jnp.sum(cached_exp, axis=1, keepdims=True)
    for value in fresh_exp:
        denominator += value
    weights = cached_exp / denominator
    mixed = jnp.zeros((cols, head), F32)
    for s in range(steps):
        share = (fresh_exp[s] / denominator).astype(BF).astype(F32)
        mixed += share * dot(spread_bf, vn_ref[s])
    loads[1].wait()
    parts = []
    for g in range(rows // group):
        values = v_buf[g * group:(g + 1) * group].reshape(group * slots, head)
        own_w = weights[g * TILE:(g + 1) * TILE]
        blocked = jnp.concatenate(
            [jnp.where(group_of == j, own_w, 0.0) for j in range(group)], axis=1
        ).astype(BF)
        parts.append(dot(blocked, values))
    mixed = (mixed + jnp.concatenate(parts, axis=0)).astype(BF)
    lines = dot(back, mixed).astype(BF)
    features = []
    for s in range(steps):
        at = s * heads * rows
        features.append(jnp.concatenate(
            [lines[at + h * rows:at + (h + 1) * rows] for h in range(heads)], axis=1
        ))

    packed = dot(one_hot(packs[0]), features[0])
    for s in range(1, steps):
        packed += dot(one_hot(packs[s]), features[s])
    packed = packed.astype(BF)
    x_s[...] = packed.reshape(n_inst, pack, width)
    x_copies = []
    for k in range(1, n_inst):
        copy = remote(x_s.at[k], x_r.at[k], x_ss.at[k], x_rs.at[k], inst_at(k))
        copy.start()
        x_copies.append(copy)
    x_r[0] = packed[:pack]

    feats = jnp.concatenate(features, axis=0)
    loads[2].wait()

    def base_part(ky, parity):
        at = (lax.rem(y + ky, n_y) * 2 + parity) * out_cols
        return dot(feats, w_buf[:, pl.ds(pl.multiple_of(at, out_cols), out_cols)])

    b1_copies = {}
    for ky in reversed(range(n_y)):
        b1_s[ky] = base_part(ky, 1 - core).astype(BF)
        copy = remote(
            b1_s.at[ky], b1_r.at[ky], b1_ss.at[ky], b1_rs.at[ky], (me, y * 2 + 1 - core)
        )
        copy.start()
        b1_copies[ky] = copy
    for ky in reversed(range(n_y)):
        own[ky] = base_part(ky, core)

    loads[3].wait()
    flat = jnp.zeros((dn_buf.shape[1], adapters * rank), F32)
    tr, tl = rows_iota((rank, adapters * rank)), lanes_iota((rank, adapters * rank))
    for a in range(adapters):
        flat += dot(dn_buf[a], one_hot(tl == tr + a * rank))
    dn_flat[...] = flat.astype(BF)
    for copy in meta_copies:
        copy.wait_recv()
    slot_got = meta_r[...].reshape(total, LANES).astype(F32)
    lane = lanes_iota((total, LANES))
    masks = [
        slot_got == ((lane + c * LANES) >> log2(rank)).astype(F32) for c in range(chunks)
    ]
    for copy in x_copies:
        copy.wait_recv()
    ranked = dot(x_r[...].reshape(total, width), dn_flat[...])
    folded = jnp.zeros((total, LANES), F32)
    for c in range(chunks):
        folded += jnp.where(masks[c], ranked[:, c * LANES:(c + 1) * LANES], 0.0)
    rk_s[...] = folded.astype(BF)
    rk_copies = []
    for k in range(1, n_tp):
        copy = remote(rk_s, rk_r.at[k], rk_ss.at[k], rk_rs.at[k], tp_at(k))
        copy.start()
        rk_copies.append(copy)

    b2_copies = []
    for ky in range(1, n_y):
        b1_copies[ky].wait_recv()
        b2_s[ky] = (own[ky] + b1_r[ky].astype(F32)).astype(BF)
        copy = remote(
            b2_s.at[ky], b2_r.at[ky], b2_ss.at[ky], b2_rs.at[ky],
            (me, lax.rem(y + ky, n_y) * 2 + core),
        )
        copy.start()
        b2_copies.append(copy)

    loads[4].wait()
    for k, copy in enumerate(rk_copies, 1):
        copy.wait_recv()
        folded += rk_r[k].astype(F32)
    wide = jnp.concatenate(
        [jnp.where(masks[c], folded, 0.0) for c in range(chunks)], axis=1
    ).astype(BF)
    delta = dot(wide, up_buf[...].reshape(adapters * rank, out_cols)).astype(BF)
    dl_s[...] = delta.reshape(n_inst, pack, out_cols)
    dl_copies = []
    for k in range(1, n_inst):
        copy = remote(dl_s.at[k], dl_r.at[k], dl_ss.at[k], dl_rs.at[k], inst_at(-k))
        copy.start()
        dl_copies.append(copy)
    dl_r[0] = delta[:pack]

    b1_copies[0].wait_recv()
    base = own[0] + b1_r[0].astype(F32)
    for ky, copy in enumerate(b2_copies, 1):
        copy.wait_recv()
        base += b2_r[ky].astype(F32)
    own[0] = base
    unpack = jnp.concatenate(
        [one_hot(lanes_iota((rows, total)) == to_col + step * cap) for step in range(steps)], axis=0
    )
    for copy in dl_copies:
        copy.wait_recv()
    result = own[0] + dot(unpack, dl_r[...].reshape(total, out_cols))
    out_ref[...] = result.astype(BF).reshape(steps, rows, out_cols)

    for copy in meta_copies + x_copies + rk_copies + b2_copies + dl_copies:
        copy.wait_send()
    for ky in range(n_y):
        b1_copies[ky].wait_send()


def shards(
    n_inst, n_tp,
    queries, stored_keys, stored_values, incoming_keys, incoming_values, cache_length_rows,
    output_matrix, adapter_down_weight, adapter_up_weight, host, slot,
):
    steps, rows, width = queries.shape
    adapters, _, rank = adapter_down_weight.shape
    out_cols = adapter_up_weight.shape[2]
    cap = max(1, 2 * rows // n_inst)
    pack = -(-steps * cap // TILE) * TILE
    total = n_inst * pack
    n_y = n_tp // 2
    lines = steps * rows
    vmem = pl.BlockSpec(memory_space=pltpu.VMEM)
    far = pl.BlockSpec(memory_space=pl.ANY)
    sem = pltpu.SemaphoreType.DMA
    return pl.pallas_call(
        functools.partial(kernel, n_inst, n_tp, cap),
        out_shape=jax.ShapeDtypeStruct((steps, rows, out_cols), BF),
        in_specs=[vmem] * 6 + [far] * 5,
        out_specs=vmem,
        scratch_shapes=[
            pltpu.VMEM(stored_keys.shape, BF),
            pltpu.VMEM(stored_values.shape, BF),
            pltpu.VMEM(output_matrix.shape, BF),
            pltpu.VMEM(adapter_down_weight.shape, BF),
            pltpu.VMEM(adapter_up_weight.shape, BF),
            pltpu.VMEM((width, adapters * rank), BF),
            pltpu.VMEM((n_inst, pack, LANES), BF),
            pltpu.VMEM((n_inst, pack, LANES), BF),
            pltpu.VMEM((n_inst, pack, width), BF),
            pltpu.VMEM((n_inst, pack, width), BF),
            pltpu.VMEM((n_inst, pack, out_cols), BF),
            pltpu.VMEM((n_inst, pack, out_cols), BF),
            pltpu.VMEM((total, LANES), BF),
            pltpu.VMEM((n_tp, total, LANES), BF),
            pltpu.VMEM((n_y, lines, out_cols), BF),
            pltpu.VMEM((n_y, lines, out_cols), BF),
            pltpu.VMEM((n_y, lines, out_cols), BF),
            pltpu.VMEM((n_y, lines, out_cols), BF),
            pltpu.VMEM((n_y, lines, out_cols), F32),
            sem((5,)),
            sem((n_inst,)), sem((n_inst,)),
            sem((n_inst,)), sem((n_inst,)),
            sem((n_inst,)), sem((n_inst,)),
            sem((n_tp,)), sem((n_tp,)),
            sem((n_y,)), sem((n_y,)),
            sem((n_y,)), sem((n_y,)),
        ],
        compiler_params=pltpu.CompilerParams(
            collective_id=0, has_side_effects=True, vmem_limit_bytes=48 * 1024 * 1024
        ),
    )(
        queries, incoming_keys, incoming_values,
        cache_length_rows.reshape(1, rows), host.reshape(1, rows), slot.reshape(1, rows),
        stored_keys, stored_values, output_matrix, adapter_down_weight, adapter_up_weight,
    )


def solution(mesh):
    return jax.shard_map(
        functools.partial(shards, mesh.shape["inst"], mesh.shape["tp"]),
        mesh=mesh,
        in_specs=(
            P(None, "inst", "tp"),
            P("inst", None, "tp"),
            P("inst", None, "tp"),
            P(None, "inst", "tp"),
            P(None, "inst", "tp"),
            P("inst"),
            P("tp", None),
            P("inst", "tp", None),
            P("inst", None, "tp"),
            P("inst", None),
            P("inst"),
        ),
        out_specs=P(None, "inst", "tp"),
        check_vma=False,
    )
```

```python
import functools
import math

import jax
import jax.numpy as jnp
from jax import lax
from jax.experimental import pallas as pl
from jax.experimental.pallas import tpu as pltpu
from jax.sharding import PartitionSpec as P

MESH = pl.DeviceIdType.MESH
BF = jnp.bfloat16
F32 = jnp.float32
TILE = 16
LANES = 128


def log2(n):
    assert n & (n - 1) == 0
    return n.bit_length() - 1


def rows_iota(shape):
    return lax.broadcasted_iota(jnp.int32, shape, 0)


def lanes_iota(shape):
    return lax.broadcasted_iota(jnp.int32, shape, 1)


def dot(a, b):
    return jnp.dot(a, b, preferred_element_type=F32)


def dot_t(a, b):
    return lax.dot_general(a, b, (((1,), (1,)), ((), ())), preferred_element_type=F32)


def one_hot(mask):
    return jnp.where(mask, 1.0, 0.0).astype(BF)


def kernel(
    n_inst, n_tp, cap,
    host_hbm, slot_hbm, q_hbm, kn_hbm, len_hbm, k_hbm, vn_hbm, v_hbm, w_hbm, dn_hbm, up_hbm,
    out_ref,
    host_ref, slot_ref, q_ref, kn_ref, len_ref, k_buf, vn_ref, v_buf, w_buf, dn_buf, up_buf,
    meta_s, meta_r, x_s, x_r, dl_s, dl_r, rk_s, rk_r,
    b1_s, b1_r, b2_s, b2_r, own,
    in_sem, meta_ss, meta_rs, x_ss, x_rs, dl_ss, dl_rs, rk_ss, rk_rs,
    b1_ss, b1_rs, b2_ss, b2_rs,
):
    steps, rows, width = q_ref.shape
    head = kn_ref.shape[2]
    heads = width // head
    slots = k_buf.shape[1]
    per_row = steps * heads
    cols = rows * per_row
    pack = meta_s.shape[1]
    total = n_inst * pack
    adapters, rank, _ = dn_buf.shape
    chunks = adapters * rank // LANES
    out_cols = up_buf.shape[2]
    n_y = n_tp // 2
    me = lax.axis_index("inst")
    tp = lax.axis_index("tp")
    y = tp // 2
    core = lax.rem(tp, 2)

    def inst_at(k):
        return (lax.rem(me + k + n_inst, n_inst), tp)

    def tp_at(k):
        return (me, lax.rem(tp + k, n_tp))

    def remote(src, dst, send, recv, where):
        return pltpu.make_async_remote_copy(
            src_ref=src, dst_ref=dst, send_sem=send, recv_sem=recv,
            device_id=where, device_id_type=MESH,
        )

    loads = []
    for at, (src, dst) in enumerate((
        (host_hbm, host_ref), (slot_hbm, slot_ref), (q_hbm, q_ref), (kn_hbm, kn_ref),
        (len_hbm, len_ref), (k_hbm, k_buf), (vn_hbm, vn_ref), (v_hbm, v_buf),
        (w_hbm, w_buf), (dn_hbm, dn_buf), (up_hbm, up_buf),
    )):
        load = pltpu.make_async_copy(src, dst, in_sem.at[at])
        load.start()
        loads.append(load)
    barrier = pltpu.get_barrier_semaphore()
    for k in range(1, n_inst):
        pl.semaphore_signal(barrier, inc=1, device_id=inst_at(k), device_id_type=MESH)
    for k in range(1, n_tp):
        pl.semaphore_signal(barrier, inc=1, device_id=tp_at(k), device_id_type=MESH)

    loads[0].wait()
    loads[1].wait()
    host_lane = host_ref[...].astype(F32)
    slot_lane = slot_ref[...].astype(F32)
    here = me.astype(F32)
    square = (rows, rows)
    ri, li = rows_iota(square), lanes_iota(square)
    host_col = jnp.sum(jnp.where(ri == li, host_lane, 0.0), axis=1, keepdims=True)
    same = jnp.broadcast_to(host_col, square) == jnp.broadcast_to(host_lane, square)
    pos_lane = jnp.sum(jnp.where(same & (ri < li), 1.0, 0.0), axis=0, keepdims=True)
    pos_col = jnp.sum(jnp.where(same & (li < ri), 1.0, 0.0), axis=1, keepdims=True)

    def place(host, pos):
        away = host - here
        away = jnp.where(away < 0.0, away + float(n_inst), away)
        return away * float(pack) + pos

    to_lane = place(host_lane, pos_lane).astype(jnp.int32)
    to_col = place(host_col, pos_col).astype(jnp.int32)
    pack_i = rows_iota((total, rows))
    packs = [pack_i == to_lane + step * cap for step in range(steps)]
    slot_packed = jnp.zeros((total, 1), F32)
    for chosen in packs:
        slot_packed += jnp.sum(jnp.where(chosen, slot_lane, 0.0), axis=1, keepdims=True)
    slot_packed = jnp.broadcast_to(slot_packed, (total, LANES)).astype(BF)
    meta_s[...] = slot_packed.reshape(n_inst, pack, LANES)
    meta_r[0] = slot_packed[:pack]

    pl.semaphore_wait(barrier, n_inst - 1 + n_tp - 1)
    meta_copies = []
    for k in range(1, n_inst):
        copy = remote(meta_s.at[k], meta_r.at[k], meta_ss.at[k], meta_rs.at[k], inst_at(k))
        copy.start()
        meta_copies.append(copy)

    ci = rows_iota((cols, cols))
    cj = lanes_iota((cols, cols))
    into = one_hot(cj == ((ci & (per_row - 1)) << log2(rows)) + (ci >> log2(per_row)))
    back = one_hot(ci == ((cj & (per_row - 1)) << log2(rows)) + (cj >> log2(per_row)))
    for load in loads[2:5]:
        load.wait()
    q_all = jnp.concatenate(
        [q_ref[s, :, h * head:(h + 1) * head] for s in range(steps) for h in range(heads)], axis=0
    )
    q_lines = dot(into, q_all)
    q_bf = q_lines.astype(BF)
    spread = rows_iota((cols, rows)) >> log2(per_row) == lanes_iota((cols, rows))
    lengths = jnp.sum(
        jnp.where(spread, len_ref[...].astype(F32), 0.0), axis=1, keepdims=True
    ).astype(jnp.int32)
    spread_bf = one_hot(spread)
    scale = 1.0 / math.sqrt(head)
    step_of = (rows_iota((cols, 1)) & (per_row - 1)) >> log2(heads)
    fresh = []
    for s in range(steps):
        value = jnp.sum(q_lines * dot(spread_bf, kn_ref[s]), axis=1, keepdims=True) * scale
        fresh.append(jnp.where(step_of >= s, value, -1e30))
    group = TILE // per_row
    group_of = rows_iota((TILE, slots)) >> log2(per_row)
    loads[5].wait()
    scores = []
    for g in range(rows // group):
        keys = k_buf[g * group:(g + 1) * group].reshape(group * slots, head)
        raw = dot_t(q_bf[g * TILE:(g + 1) * TILE], keys)
        picked = raw[:, :slots]
        for j in range(1, group):
            picked = jnp.where(group_of == j, raw[:, j * slots:(j + 1) * slots], picked)
        scores.append(picked)
    scores = jnp.concatenate(scores, axis=0) * scale
    scores = jnp.where(lanes_iota((cols, slots)) < lengths, scores, -1e30)
    highest = jnp.max(scores, axis=1, keepdims=True)
    for value in fresh:
        highest = jnp.maximum(highest, value)
    cached_exp = jnp.exp(scores - highest)
    fresh_exp = [jnp.exp(value - highest) for value in fresh]
    denominator = jnp.sum(cached_exp, axis=1, keepdims=True)
    for value in fresh_exp:
        denominator += value
    weights = cached_exp / denominator
    mixed = jnp.zeros((cols, head), F32)
    loads[6].wait()
    for s in range(steps):
        share = (fresh_exp[s] / denominator).astype(BF).astype(F32)
        mixed += share * dot(spread_bf, vn_ref[s])
    loads[7].wait()
    parts = []
    for g in range(rows // group):
        values = v_buf[g * group:(g + 1) * group].reshape(group * slots, head)
        own_w = weights[g * TILE:(g + 1) * TILE]
        blocked = jnp.concatenate(
            [jnp.where(group_of == j, own_w, 0.0) for j in range(group)], axis=1
        ).astype(BF)
        parts.append(dot(blocked, values))
    mixed = (mixed + jnp.concatenate(parts, axis=0)).astype(BF)
    lines = dot(back, mixed).astype(BF)
    features = []
    for s in range(steps):
        at = s * heads * rows
        features.append(jnp.concatenate(
            [lines[at + h * rows:at + (h + 1) * rows] for h in range(heads)], axis=1
        ))

    packed = dot(one_hot(packs[0]), features[0])
    for s in range(1, steps):
        packed += dot(one_hot(packs[s]), features[s])
    packed = packed.astype(BF)
    x_s[...] = packed.reshape(n_inst, pack, width)
    x_copies = []
    for k in range(1, n_inst):
        copy = remote(x_s.at[k], x_r.at[k], x_ss.at[k], x_rs.at[k], inst_at(k))
        copy.start()
        x_copies.append(copy)
    x_r[0] = packed[:pack]

    feats = jnp.concatenate(features, axis=0)
    loads[8].wait()

    def base_part(ky, parity):
        at = (lax.rem(y + ky, n_y) * 2 + parity) * out_cols
        return dot(feats, w_buf[:, pl.ds(pl.multiple_of(at, out_cols), out_cols)])

    b1_copies = {}
    for ky in reversed(range(n_y)):
        b1_s[ky] = base_part(ky, 1 - core).astype(BF)
        copy = remote(
            b1_s.at[ky], b1_r.at[ky], b1_ss.at[ky], b1_rs.at[ky], (me, y * 2 + 1 - core)
        )
        copy.start()
        b1_copies[ky] = copy
    for ky in reversed(range(n_y)):
        own[ky] = base_part(ky, core)

    loads[9].wait()
    for copy in meta_copies:
        copy.wait_recv()
    slot_got = meta_r[...].reshape(total, LANES).astype(F32)
    lane = lanes_iota((total, LANES))
    masks = [
        slot_got == ((lane + c * LANES) >> log2(rank)).astype(F32) for c in range(chunks)
    ]
    for copy in x_copies:
        copy.wait_recv()
    ranked = dot_t(
        x_r[...].reshape(total, width), dn_buf[...].reshape(adapters * rank, width)
    )
    folded = jnp.zeros((total, LANES), F32)
    for c in range(chunks):
        folded += jnp.where(masks[c], ranked[:, c * LANES:(c + 1) * LANES], 0.0)
    rk_s[...] = folded.astype(BF)
    rk_copies = []
    for k in range(1, n_tp):
        copy = remote(rk_s, rk_r.at[k], rk_ss.at[k], rk_rs.at[k], tp_at(k))
        copy.start()
        rk_copies.append(copy)

    b2_copies = []
    for ky in range(1, n_y):
        b1_copies[ky].wait_recv()
        b2_s[ky] = (own[ky] + b1_r[ky].astype(F32)).astype(BF)
        copy = remote(
            b2_s.at[ky], b2_r.at[ky], b2_ss.at[ky], b2_rs.at[ky],
            (me, lax.rem(y + ky, n_y) * 2 + core),
        )
        copy.start()
        b2_copies.append(copy)

    loads[10].wait()
    for k, copy in enumerate(rk_copies, 1):
        copy.wait_recv()
        folded += rk_r[k].astype(F32)
    wide = jnp.concatenate(
        [jnp.where(masks[c], folded, 0.0) for c in range(chunks)], axis=1
    ).astype(BF)
    delta = dot(wide, up_buf[...].reshape(adapters * rank, out_cols)).astype(BF)
    dl_s[...] = delta.reshape(n_inst, pack, out_cols)
    dl_copies = []
    for k in range(1, n_inst):
        copy = remote(dl_s.at[k], dl_r.at[k], dl_ss.at[k], dl_rs.at[k], inst_at(-k))
        copy.start()
        dl_copies.append(copy)
    dl_r[0] = delta[:pack]

    b1_copies[0].wait_recv()
    base = own[0] + b1_r[0].astype(F32)
    for ky, copy in enumerate(b2_copies, 1):
        copy.wait_recv()
        base += b2_r[ky].astype(F32)
    own[0] = base
    unpack = jnp.concatenate(
        [one_hot(lanes_iota((rows, total)) == to_col + step * cap) for step in range(steps)], axis=0
    )
    for copy in dl_copies:
        copy.wait_recv()
    result = own[0] + dot(unpack, dl_r[...].reshape(total, out_cols))
    out_ref[...] = result.astype(BF).reshape(steps, rows, out_cols)

    for copy in meta_copies + x_copies + rk_copies + b2_copies + dl_copies:
        copy.wait_send()
    for ky in range(n_y):
        b1_copies[ky].wait_send()


def shards(
    n_inst, n_tp,
    queries, stored_keys, stored_values, incoming_keys, incoming_values, cache_length_rows,
    output_matrix, adapter_down_weight, adapter_up_weight, host, slot,
):
    steps, rows, width = queries.shape
    adapters, _, rank = adapter_down_weight.shape
    out_cols = adapter_up_weight.shape[2]
    cap = max(1, 2 * rows // n_inst)
    pack = -(-steps * cap // TILE) * TILE
    total = n_inst * pack
    n_y = n_tp // 2
    lines = steps * rows
    operands = (
        host.reshape(1, rows), slot.reshape(1, rows), queries, incoming_keys,
        cache_length_rows.reshape(1, rows), stored_keys, incoming_values, stored_values,
        output_matrix, jnp.swapaxes(adapter_down_weight, 1, 2), adapter_up_weight,
    )
    vmem = pl.BlockSpec(memory_space=pltpu.VMEM)
    far = pl.BlockSpec(memory_space=pltpu.HBM)
    sem = pltpu.SemaphoreType.DMA
    return pl.pallas_call(
        functools.partial(kernel, n_inst, n_tp, cap),
        out_shape=jax.ShapeDtypeStruct((steps, rows, out_cols), BF),
        in_specs=[far] * len(operands),
        out_specs=vmem,
        scratch_shapes=[
            *[pltpu.VMEM(operand.shape, operand.dtype) for operand in operands],
            pltpu.VMEM((n_inst, pack, LANES), BF),
            pltpu.VMEM((n_inst, pack, LANES), BF),
            pltpu.VMEM((n_inst, pack, width), BF),
            pltpu.VMEM((n_inst, pack, width), BF),
            pltpu.VMEM((n_inst, pack, out_cols), BF),
            pltpu.VMEM((n_inst, pack, out_cols), BF),
            pltpu.VMEM((total, LANES), BF),
            pltpu.VMEM((n_tp, total, LANES), BF),
            pltpu.VMEM((n_y, lines, out_cols), BF),
            pltpu.VMEM((n_y, lines, out_cols), BF),
            pltpu.VMEM((n_y, lines, out_cols), BF),
            pltpu.VMEM((n_y, lines, out_cols), BF),
            pltpu.VMEM((n_y, lines, out_cols), F32),
            sem((len(operands),)),
            sem((n_inst,)), sem((n_inst,)),
            sem((n_inst,)), sem((n_inst,)),
            sem((n_inst,)), sem((n_inst,)),
            sem((n_tp,)), sem((n_tp,)),
            sem((n_y,)), sem((n_y,)),
            sem((n_y,)), sem((n_y,)),
        ],
        compiler_params=pltpu.CompilerParams(
            collective_id=0, has_side_effects=True, vmem_limit_bytes=60 * 1024 * 1024
        ),
    )(*operands)


def solution(mesh):
    return jax.shard_map(
        functools.partial(shards, mesh.shape["inst"], mesh.shape["tp"]),
        mesh=mesh,
        in_specs=(
            P(None, "inst", "tp"),
            P("inst", None, "tp"),
            P("inst", None, "tp"),
            P(None, "inst", "tp"),
            P(None, "inst", "tp"),
            P("inst"),
            P("tp", None),
            P("inst", "tp", None),
            P("inst", None, "tp"),
            P("inst", None),
            P("inst"),
        ),
        out_specs=P(None, "inst", "tp"),
        check_vma=False,
    )
```

```python
import functools
import math

import jax
import jax.numpy as jnp
from jax import lax
from jax.experimental import pallas as pl
from jax.experimental.pallas import tpu as pltpu
from jax.sharding import PartitionSpec as P

MESH = pl.DeviceIdType.MESH
BF = jnp.bfloat16
F32 = jnp.float32
TILE = 16
LANES = 128


def log2(n):
    assert n & (n - 1) == 0
    return n.bit_length() - 1


def rows_iota(shape):
    return lax.broadcasted_iota(jnp.int32, shape, 0)


def lanes_iota(shape):
    return lax.broadcasted_iota(jnp.int32, shape, 1)


def dot(a, b):
    return jnp.dot(a, b, preferred_element_type=F32)


def dot_t(a, b):
    return lax.dot_general(a, b, (((1,), (1,)), ((), ())), preferred_element_type=F32)


def one_hot(mask):
    return jnp.where(mask, 1.0, 0.0).astype(BF)


def kernel(
    n_inst, n_tp, cap,
    host_hbm, slot_hbm, q_hbm, kn_hbm, len_hbm, k_hbm, vn_hbm, v_hbm, w_hbm, dn_hbm, up_hbm,
    out_ref,
    host_ref, slot_ref, q_ref, kn_ref, len_ref, k_buf, vn_ref, v_buf, w_buf, dn_buf, up_buf,
    x_s, x_r, dl_s, dl_r, rk_s, rk_r,
    b1_s, b1_r, b2_s, b2_r, own,
    in_sem, x_ss, x_rs, dl_ss, dl_rs, rk_ss, rk_rs,
    b1_ss, b1_rs, b2_ss, b2_rs,
):
    steps, rows, width = q_ref.shape
    head = kn_ref.shape[2]
    heads = width // head
    slots = k_buf.shape[1]
    per_row = steps * heads
    cols = rows * per_row
    pack = x_s.shape[1]
    total = n_inst * pack
    adapters, rank, _ = dn_buf.shape
    chunks = adapters * rank // LANES
    out_cols = up_buf.shape[2]
    n_y = n_tp // 2
    me = lax.axis_index("inst")
    tp = lax.axis_index("tp")
    y = tp // 2
    core = lax.rem(tp, 2)

    def inst_at(k):
        return (lax.rem(me + k + n_inst, n_inst), tp)

    def tp_at(k):
        return (me, lax.rem(tp + k, n_tp))

    def remote(src, dst, send, recv, where):
        return pltpu.make_async_remote_copy(
            src_ref=src, dst_ref=dst, send_sem=send, recv_sem=recv,
            device_id=where, device_id_type=MESH,
        )

    far_first = sorted(range(1, n_inst), key=lambda k: -min(k, n_inst - k))
    loads = []
    for at, (src, dst) in enumerate((
        (host_hbm, host_ref), (slot_hbm, slot_ref), (q_hbm, q_ref), (kn_hbm, kn_ref),
        (len_hbm, len_ref), (k_hbm, k_buf), (vn_hbm, vn_ref), (v_hbm, v_buf),
        (w_hbm, w_buf), (dn_hbm, dn_buf), (up_hbm, up_buf),
    )):
        load = pltpu.make_async_copy(src, dst, in_sem.at[at])
        load.start()
        loads.append(load)
    barrier = pltpu.get_barrier_semaphore()
    for k in range(1, n_inst):
        pl.semaphore_signal(barrier, inc=1, device_id=inst_at(k), device_id_type=MESH)
    for k in range(1, n_tp):
        pl.semaphore_signal(barrier, inc=1, device_id=tp_at(k), device_id_type=MESH)

    loads[0].wait()
    loads[1].wait()
    host_lane = host_ref[...].astype(F32)
    slot_lane = slot_ref[...].astype(F32)
    here = me.astype(F32)
    square = (rows, rows)
    ri, li = rows_iota(square), lanes_iota(square)
    host_col = jnp.sum(jnp.where(ri == li, host_lane, 0.0), axis=1, keepdims=True)
    same = jnp.broadcast_to(host_col, square) == jnp.broadcast_to(host_lane, square)
    pos_lane = jnp.sum(jnp.where(same & (ri < li), 1.0, 0.0), axis=0, keepdims=True)
    pos_col = jnp.sum(jnp.where(same & (li < ri), 1.0, 0.0), axis=1, keepdims=True)

    def place(host, pos):
        away = host - here
        away = jnp.where(away < 0.0, away + float(n_inst), away)
        return away * float(pack) + pos

    to_lane = place(host_lane, pos_lane).astype(jnp.int32)
    to_col = place(host_col, pos_col).astype(jnp.int32)
    pack_i = rows_iota((total, rows))
    packs = [pack_i == to_lane + step * cap for step in range(steps)]
    slot_packed = jnp.zeros((total, 1), F32)
    for chosen in packs:
        slot_packed += jnp.sum(jnp.where(chosen, slot_lane, 0.0), axis=1, keepdims=True)
    slot_packed = jnp.broadcast_to(slot_packed, (total, LANES)).astype(BF)
    x_s[:, :, width:] = slot_packed.reshape(n_inst, pack, LANES)
    x_r[0, :, width:] = slot_packed[:pack]

    ci = rows_iota((cols, cols))
    cj = lanes_iota((cols, cols))
    into = one_hot(cj == ((ci & (per_row - 1)) << log2(rows)) + (ci >> log2(per_row)))
    back = one_hot(ci == ((cj & (per_row - 1)) << log2(rows)) + (cj >> log2(per_row)))
    for load in loads[2:5]:
        load.wait()
    q_all = jnp.concatenate(
        [q_ref[s, :, h * head:(h + 1) * head] for s in range(steps) for h in range(heads)], axis=0
    )
    q_lines = dot(into, q_all)
    q_bf = q_lines.astype(BF)
    spread = rows_iota((cols, rows)) >> log2(per_row) == lanes_iota((cols, rows))
    lengths = jnp.sum(
        jnp.where(spread, len_ref[...].astype(F32), 0.0), axis=1, keepdims=True
    ).astype(jnp.int32)
    spread_bf = one_hot(spread)
    scale = 1.0 / math.sqrt(head)
    step_of = (rows_iota((cols, 1)) & (per_row - 1)) >> log2(heads)
    fresh = []
    for s in range(steps):
        value = jnp.sum(q_lines * dot(spread_bf, kn_ref[s]), axis=1, keepdims=True) * scale
        fresh.append(jnp.where(step_of >= s, value, -1e30))
    group = TILE // per_row
    group_of = rows_iota((TILE, slots)) >> log2(per_row)
    loads[5].wait()
    scores = []
    for g in range(rows // group):
        keys = k_buf[g * group:(g + 1) * group].reshape(group * slots, head)
        raw = dot_t(q_bf[g * TILE:(g + 1) * TILE], keys)
        picked = raw[:, :slots]
        for j in range(1, group):
            picked = jnp.where(group_of == j, raw[:, j * slots:(j + 1) * slots], picked)
        scores.append(picked)
    scores = jnp.concatenate(scores, axis=0) * scale
    scores = jnp.where(lanes_iota((cols, slots)) < lengths, scores, -1e30)
    highest = jnp.max(scores, axis=1, keepdims=True)
    for value in fresh:
        highest = jnp.maximum(highest, value)
    cached_exp = jnp.exp(scores - highest)
    fresh_exp = [jnp.exp(value - highest) for value in fresh]
    denominator = jnp.sum(cached_exp, axis=1, keepdims=True)
    for value in fresh_exp:
        denominator += value
    weights = cached_exp / denominator
    mixed = jnp.zeros((cols, head), F32)
    loads[6].wait()
    for s in range(steps):
        share = (fresh_exp[s] / denominator).astype(BF).astype(F32)
        mixed += share * dot(spread_bf, vn_ref[s])
    loads[7].wait()
    parts = []
    for g in range(rows // group):
        values = v_buf[g * group:(g + 1) * group].reshape(group * slots, head)
        own_w = weights[g * TILE:(g + 1) * TILE]
        blocked = jnp.concatenate(
            [jnp.where(group_of == j, own_w, 0.0) for j in range(group)], axis=1
        ).astype(BF)
        parts.append(dot(blocked, values))
    mixed = (mixed + jnp.concatenate(parts, axis=0)).astype(BF)
    lines = dot(back, mixed).astype(BF)
    features = []
    for s in range(steps):
        at = s * heads * rows
        features.append(jnp.concatenate(
            [lines[at + h * rows:at + (h + 1) * rows] for h in range(heads)], axis=1
        ))

    packed = dot(one_hot(packs[0]), features[0])
    for s in range(1, steps):
        packed += dot(one_hot(packs[s]), features[s])
    packed = packed.astype(BF)
    x_s[:, :, :width] = packed.reshape(n_inst, pack, width)
    pl.semaphore_wait(barrier, n_inst - 1 + n_tp - 1)
    x_copies = []
    for k in far_first:
        copy = remote(x_s.at[k], x_r.at[k], x_ss.at[k], x_rs.at[k], inst_at(k))
        copy.start()
        x_copies.append(copy)
    x_r[0, :, :width] = packed[:pack]

    feats = jnp.concatenate(features, axis=0)
    loads[8].wait()

    def base_part(ky, parity):
        at = (lax.rem(y + ky, n_y) * 2 + parity) * out_cols
        return dot(feats, w_buf[:, pl.ds(pl.multiple_of(at, out_cols), out_cols)])

    b1_copies = {}
    for ky in reversed(range(n_y)):
        b1_s[ky] = base_part(ky, 1 - core).astype(BF)
        copy = remote(
            b1_s.at[ky], b1_r.at[ky], b1_ss.at[ky], b1_rs.at[ky], (me, y * 2 + 1 - core)
        )
        copy.start()
        b1_copies[ky] = copy
    loads[9].wait()
    for copy in x_copies:
        copy.wait_recv()
    slot_got = x_r[:, :, width:].reshape(total, LANES).astype(F32)
    lane = lanes_iota((total, LANES))
    masks = [
        slot_got == ((lane + c * LANES) >> log2(rank)).astype(F32) for c in range(chunks)
    ]
    ranked = dot_t(
        x_r[:, :, :width].reshape(total, width), dn_buf[...].reshape(adapters * rank, width)
    )
    folded = jnp.zeros((total, LANES), F32)
    for c in range(chunks):
        folded += jnp.where(masks[c], ranked[:, c * LANES:(c + 1) * LANES], 0.0)
    rk_s[...] = folded.astype(BF)
    rk_copies = []
    for k in range(1, n_tp):
        copy = remote(rk_s, rk_r.at[k], rk_ss.at[k], rk_rs.at[k], tp_at(k))
        copy.start()
        rk_copies.append(copy)

    for ky in reversed(range(n_y)):
        own[ky] = base_part(ky, core)
    b2_copies = []
    for ky in range(1, n_y):
        b1_copies[ky].wait_recv()
        b2_s[ky] = (own[ky] + b1_r[ky].astype(F32)).astype(BF)
        copy = remote(
            b2_s.at[ky], b2_r.at[ky], b2_ss.at[ky], b2_rs.at[ky],
            (me, lax.rem(y + ky, n_y) * 2 + core),
        )
        copy.start()
        b2_copies.append(copy)

    loads[10].wait()
    for k, copy in enumerate(rk_copies, 1):
        copy.wait_recv()
        folded += rk_r[k].astype(F32)
    wide = jnp.concatenate(
        [jnp.where(masks[c], folded, 0.0) for c in range(chunks)], axis=1
    ).astype(BF)
    delta = dot(wide, up_buf[...].reshape(adapters * rank, out_cols)).astype(BF)
    dl_s[...] = delta.reshape(n_inst, pack, out_cols)
    dl_copies = []
    for k in far_first:
        copy = remote(dl_s.at[k], dl_r.at[k], dl_ss.at[k], dl_rs.at[k], inst_at(-k))
        copy.start()
        dl_copies.append(copy)
    dl_r[0] = delta[:pack]

    b1_copies[0].wait_recv()
    base = own[0] + b1_r[0].astype(F32)
    for ky, copy in enumerate(b2_copies, 1):
        copy.wait_recv()
        base += b2_r[ky].astype(F32)
    own[0] = base
    unpack = jnp.concatenate(
        [one_hot(lanes_iota((rows, total)) == to_col + step * cap) for step in range(steps)], axis=0
    )
    for copy in dl_copies:
        copy.wait_recv()
    result = own[0] + dot(unpack, dl_r[...].reshape(total, out_cols))
    out_ref[...] = result.astype(BF).reshape(steps, rows, out_cols)

    for copy in x_copies + rk_copies + b2_copies + dl_copies:
        copy.wait_send()
    for ky in range(n_y):
        b1_copies[ky].wait_send()


def shards(
    n_inst, n_tp,
    queries, stored_keys, stored_values, incoming_keys, incoming_values, cache_length_rows,
    output_matrix, adapter_down_weight, adapter_up_weight, host, slot,
):
    steps, rows, width = queries.shape
    adapters, _, rank = adapter_down_weight.shape
    out_cols = adapter_up_weight.shape[2]
    cap = max(1, 2 * rows // n_inst)
    pack = -(-steps * cap // TILE) * TILE
    total = n_inst * pack
    n_y = n_tp // 2
    lines = steps * rows
    operands = (
        host.reshape(1, rows), slot.reshape(1, rows), queries, incoming_keys,
        cache_length_rows.reshape(1, rows), stored_keys, incoming_values, stored_values,
        output_matrix, jnp.swapaxes(adapter_down_weight, 1, 2), adapter_up_weight,
    )
    vmem = pl.BlockSpec(memory_space=pltpu.VMEM)
    far = pl.BlockSpec(memory_space=pltpu.HBM)
    sem = pltpu.SemaphoreType.DMA
    return pl.pallas_call(
        functools.partial(kernel, n_inst, n_tp, cap),
        out_shape=jax.ShapeDtypeStruct((steps, rows, out_cols), BF),
        in_specs=[far] * len(operands),
        out_specs=vmem,
        scratch_shapes=[
            *[pltpu.VMEM(operand.shape, operand.dtype) for operand in operands],
            pltpu.VMEM((n_inst, pack, width + LANES), BF),
            pltpu.VMEM((n_inst, pack, width + LANES), BF),
            pltpu.VMEM((n_inst, pack, out_cols), BF),
            pltpu.VMEM((n_inst, pack, out_cols), BF),
            pltpu.VMEM((total, LANES), BF),
            pltpu.VMEM((n_tp, total, LANES), BF),
            pltpu.VMEM((n_y, lines, out_cols), BF),
            pltpu.VMEM((n_y, lines, out_cols), BF),
            pltpu.VMEM((n_y, lines, out_cols), BF),
            pltpu.VMEM((n_y, lines, out_cols), BF),
            pltpu.VMEM((n_y, lines, out_cols), F32),
            sem((len(operands),)),
            sem((n_inst,)), sem((n_inst,)),
            sem((n_inst,)), sem((n_inst,)),
            sem((n_tp,)), sem((n_tp,)),
            sem((n_y,)), sem((n_y,)),
            sem((n_y,)), sem((n_y,)),
        ],
        compiler_params=pltpu.CompilerParams(
            collective_id=0, has_side_effects=True, vmem_limit_bytes=60 * 1024 * 1024
        ),
    )(*operands)


def solution(mesh):
    return jax.shard_map(
        functools.partial(shards, mesh.shape["inst"], mesh.shape["tp"]),
        mesh=mesh,
        in_specs=(
            P(None, "inst", "tp"),
            P("inst", None, "tp"),
            P("inst", None, "tp"),
            P(None, "inst", "tp"),
            P(None, "inst", "tp"),
            P("inst"),
            P("tp", None),
            P("inst", "tp", None),
            P("inst", None, "tp"),
            P("inst", None),
            P("inst"),
        ),
        out_specs=P(None, "inst", "tp"),
        check_vma=False,
    )
```

```python
import functools
import math

import jax
import jax.numpy as jnp
from jax import lax
from jax.experimental import pallas as pl
from jax.experimental.pallas import tpu as pltpu
from jax.sharding import PartitionSpec as P

MESH = pl.DeviceIdType.MESH
BF = jnp.bfloat16
F32 = jnp.float32
TILE = 16
LANES = 128


def log2(n):
    assert n & (n - 1) == 0
    return n.bit_length() - 1


def rows_iota(shape):
    return lax.broadcasted_iota(jnp.int32, shape, 0)


def lanes_iota(shape):
    return lax.broadcasted_iota(jnp.int32, shape, 1)


def dot(a, b):
    return jnp.dot(a, b, preferred_element_type=F32)


def dot_t(a, b):
    return lax.dot_general(a, b, (((1,), (1,)), ((), ())), preferred_element_type=F32)


def one_hot(mask):
    return jnp.where(mask, 1.0, 0.0).astype(BF)


def kernel(
    n_inst, n_tp, cap,
    host_hbm, slot_hbm, q_hbm, kn_hbm, len_hbm, k_hbm, vn_hbm, v_hbm, w_hbm, dn_hbm, up_hbm,
    out_ref,
    host_ref, slot_ref, q_ref, kn_ref, len_ref, k_buf, vn_ref, v_buf, w_buf, dn_buf, up_buf,
    x_s, x_r, dl_s, dl_r, rk_s, rk_r,
    b1_s, b1_r, b2_s, b2_r, own,
    in_sem, x_ss, x_rs, dl_ss, dl_rs, rk_ss, rk_rs,
    b1_ss, b1_rs, b2_ss, b2_rs,
):
    steps, rows, width = q_ref.shape
    head = kn_ref.shape[2]
    heads = width // head
    slots = k_buf.shape[1]
    per_row = steps * heads
    cols = rows * per_row
    pack = x_s.shape[1]
    total = n_inst * pack
    adapters, rank, _ = dn_buf.shape
    assert 2 * rank == LANES
    chunks = adapters * rank // LANES
    out_cols = up_buf.shape[2]
    n_y = n_tp // 2
    me = lax.axis_index("inst")
    tp = lax.axis_index("tp")
    y = tp // 2
    core = lax.rem(tp, 2)

    def inst_at(k):
        return (lax.rem(me + k + n_inst, n_inst), tp)

    def tp_at(k):
        return (me, lax.rem(tp + k, n_tp))

    def remote(src, dst, send, recv, where):
        return pltpu.make_async_remote_copy(
            src_ref=src, dst_ref=dst, send_sem=send, recv_sem=recv,
            device_id=where, device_id_type=MESH,
        )

    far_first = sorted(range(1, n_inst), key=lambda k: -min(k, n_inst - k))
    loads = []
    for at, (src, dst) in enumerate((
        (host_hbm, host_ref), (slot_hbm, slot_ref), (q_hbm, q_ref), (kn_hbm, kn_ref),
        (len_hbm, len_ref), (k_hbm, k_buf), (vn_hbm, vn_ref), (v_hbm, v_buf),
        (w_hbm, w_buf), (dn_hbm, dn_buf), (up_hbm, up_buf),
    )):
        load = pltpu.make_async_copy(src, dst, in_sem.at[at])
        if at < 8:
            load.start()
        loads.append(load)
    barrier = pltpu.get_barrier_semaphore()
    for k in range(1, n_inst):
        pl.semaphore_signal(barrier, inc=1, device_id=inst_at(k), device_id_type=MESH)
    for k in range(1, n_tp):
        pl.semaphore_signal(barrier, inc=1, device_id=tp_at(k), device_id_type=MESH)

    loads[0].wait()
    loads[1].wait()
    host_lane = host_ref[...].astype(F32)
    slot_lane = slot_ref[...].astype(F32)
    here = me.astype(F32)
    square = (rows, rows)
    ri, li = rows_iota(square), lanes_iota(square)
    host_col = jnp.sum(jnp.where(ri == li, host_lane, 0.0), axis=1, keepdims=True)
    same = jnp.broadcast_to(host_col, square) == jnp.broadcast_to(host_lane, square)
    pos_lane = jnp.sum(jnp.where(same & (ri < li), 1.0, 0.0), axis=0, keepdims=True)
    pos_col = jnp.sum(jnp.where(same & (li < ri), 1.0, 0.0), axis=1, keepdims=True)

    def place(host, pos):
        away = host - here
        away = jnp.where(away < 0.0, away + float(n_inst), away)
        return away * float(pack) + pos

    to_lane = place(host_lane, pos_lane).astype(jnp.int32)
    to_col = place(host_col, pos_col).astype(jnp.int32)
    pack_i = rows_iota((total, rows))
    packs = [pack_i == to_lane + step * cap for step in range(steps)]
    slot_packed = jnp.zeros((total, 1), F32)
    for chosen in packs:
        slot_packed += jnp.sum(jnp.where(chosen, slot_lane, 0.0), axis=1, keepdims=True)
    slot_packed = jnp.broadcast_to(slot_packed, (total, LANES)).astype(BF)
    x_s[:, :, width:] = slot_packed.reshape(n_inst, pack, LANES)
    x_r[0, :, width:] = slot_packed[:pack]

    ci = rows_iota((cols, cols))
    cj = lanes_iota((cols, cols))
    into = one_hot(cj == ((ci & (per_row - 1)) << log2(rows)) + (ci >> log2(per_row)))
    back = one_hot(ci == ((cj & (per_row - 1)) << log2(rows)) + (cj >> log2(per_row)))
    for load in loads[2:5]:
        load.wait()
    q_all = jnp.concatenate(
        [q_ref[s, :, h * head:(h + 1) * head] for s in range(steps) for h in range(heads)], axis=0
    )
    q_lines = dot(into, q_all)
    q_bf = q_lines.astype(BF)
    spread = rows_iota((cols, rows)) >> log2(per_row) == lanes_iota((cols, rows))
    lengths = jnp.sum(
        jnp.where(spread, len_ref[...].astype(F32), 0.0), axis=1, keepdims=True
    ).astype(jnp.int32)
    spread_bf = one_hot(spread)
    scale = 1.0 / math.sqrt(head)
    step_of = (rows_iota((cols, 1)) & (per_row - 1)) >> log2(heads)
    fresh = []
    for s in range(steps):
        value = jnp.sum(q_lines * dot(spread_bf, kn_ref[s]), axis=1, keepdims=True) * scale
        fresh.append(jnp.where(step_of >= s, value, -1e30))
    group = TILE // per_row
    group_of = rows_iota((TILE, slots)) >> log2(per_row)
    loads[5].wait()
    for load in loads[8:]:
        load.start()
    scores = []
    for g in range(rows // group):
        keys = k_buf[g * group:(g + 1) * group].reshape(group * slots, head)
        raw = dot_t(q_bf[g * TILE:(g + 1) * TILE], keys)
        picked = raw[:, :slots]
        for j in range(1, group):
            picked = jnp.where(group_of == j, raw[:, j * slots:(j + 1) * slots], picked)
        scores.append(picked)
    scores = jnp.concatenate(scores, axis=0) * scale
    scores = jnp.where(lanes_iota((cols, slots)) < lengths, scores, -1e30)
    highest = jnp.max(scores, axis=1, keepdims=True)
    for value in fresh:
        highest = jnp.maximum(highest, value)
    cached_exp = jnp.exp(scores - highest)
    fresh_exp = [jnp.exp(value - highest) for value in fresh]
    denominator = jnp.sum(cached_exp, axis=1, keepdims=True)
    for value in fresh_exp:
        denominator += value
    weights = cached_exp / denominator
    mixed = jnp.zeros((cols, head), F32)
    loads[6].wait()
    for s in range(steps):
        share = (fresh_exp[s] / denominator).astype(BF).astype(F32)
        mixed += share * dot(spread_bf, vn_ref[s])
    loads[7].wait()
    parts = []
    for g in range(rows // group):
        values = v_buf[g * group:(g + 1) * group].reshape(group * slots, head)
        own_w = weights[g * TILE:(g + 1) * TILE]
        blocked = jnp.concatenate(
            [jnp.where(group_of == j, own_w, 0.0) for j in range(group)], axis=1
        ).astype(BF)
        parts.append(dot(blocked, values))
    mixed = (mixed + jnp.concatenate(parts, axis=0)).astype(BF)
    lines = dot(back, mixed).astype(BF)
    features = []
    for s in range(steps):
        at = s * heads * rows
        features.append(jnp.concatenate(
            [lines[at + h * rows:at + (h + 1) * rows] for h in range(heads)], axis=1
        ))

    packed = dot(one_hot(packs[0]), features[0])
    for s in range(1, steps):
        packed += dot(one_hot(packs[s]), features[s])
    packed = packed.astype(BF)
    x_s[:, :, :width] = packed.reshape(n_inst, pack, width)
    pl.semaphore_wait(barrier, n_inst - 1 + n_tp - 1)
    x_copies = []
    for k in far_first:
        copy = remote(x_s.at[k], x_r.at[k], x_ss.at[k], x_rs.at[k], inst_at(k))
        copy.start()
        x_copies.append(copy)
    x_r[0, :, :width] = packed[:pack]

    feats = jnp.concatenate(features, axis=0)
    loads[8].wait()

    def base_part(ky, parity):
        at = (lax.rem(y + ky, n_y) * 2 + parity) * out_cols
        return dot(feats, w_buf[:, pl.ds(pl.multiple_of(at, out_cols), out_cols)])

    b1_copies = {}
    for ky in reversed(range(n_y)):
        b1_s[ky] = base_part(ky, 1 - core).astype(BF)
        copy = remote(
            b1_s.at[ky], b1_r.at[ky], b1_ss.at[ky], b1_rs.at[ky], (me, y * 2 + 1 - core)
        )
        copy.start()
        b1_copies[ky] = copy
    loads[9].wait()
    for copy in x_copies:
        copy.wait_recv()
    slot_got = x_r[:, :, width:].reshape(total, LANES).astype(F32)
    lane = lanes_iota((total, LANES))
    masks = [
        slot_got == ((lane + c * LANES) >> log2(rank)).astype(F32) for c in range(chunks)
    ]
    ranked = dot_t(
        x_r[:, :, :width].reshape(total, width), dn_buf[...].reshape(adapters * rank, width)
    )
    folded = jnp.zeros((total, LANES), F32)
    for c in range(chunks):
        folded += jnp.where(masks[c], ranked[:, c * LANES:(c + 1) * LANES], 0.0)
    half = total // 2
    left = lanes_iota((half, LANES)) < rank
    both = folded + pltpu.roll(folded, LANES - rank, 1)
    paired = jnp.where(left, both[:half], both[half:])
    rk_s[...] = paired.astype(BF)
    rk_copies = []
    for k in range(1, n_tp):
        copy = remote(rk_s, rk_r.at[k], rk_ss.at[k], rk_rs.at[k], tp_at(k))
        copy.start()
        rk_copies.append(copy)

    for ky in reversed(range(n_y)):
        own[ky] = base_part(ky, core)
    b2_copies = []
    for ky in range(1, n_y):
        b1_copies[ky].wait_recv()
        b2_s[ky] = (own[ky] + b1_r[ky].astype(F32)).astype(BF)
        copy = remote(
            b2_s.at[ky], b2_r.at[ky], b2_ss.at[ky], b2_rs.at[ky],
            (me, lax.rem(y + ky, n_y) * 2 + core),
        )
        copy.start()
        b2_copies.append(copy)

    loads[10].wait()
    for k, copy in enumerate(rk_copies, 1):
        copy.wait_recv()
        paired += rk_r[k].astype(F32)
    turned = pltpu.roll(paired, LANES - rank, 1)
    folded = jnp.concatenate(
        [jnp.where(left, paired, turned), jnp.where(left, turned, paired)], axis=0
    )
    wide = jnp.concatenate(
        [jnp.where(masks[c], folded, 0.0) for c in range(chunks)], axis=1
    ).astype(BF)
    delta = dot(wide, up_buf[...].reshape(adapters * rank, out_cols)).astype(BF)
    dl_s[...] = delta.reshape(n_inst, pack, out_cols)
    dl_copies = []
    for k in far_first:
        copy = remote(dl_s.at[k], dl_r.at[k], dl_ss.at[k], dl_rs.at[k], inst_at(-k))
        copy.start()
        dl_copies.append(copy)
    dl_r[0] = delta[:pack]

    b1_copies[0].wait_recv()
    base = own[0] + b1_r[0].astype(F32)
    for ky, copy in enumerate(b2_copies, 1):
        copy.wait_recv()
        base += b2_r[ky].astype(F32)
    own[0] = base
    unpack = jnp.concatenate(
        [one_hot(lanes_iota((rows, total)) == to_col + step * cap) for step in range(steps)], axis=0
    )
    for copy in dl_copies:
        copy.wait_recv()
    result = own[0] + dot(unpack, dl_r[...].reshape(total, out_cols))
    out_ref[...] = result.astype(BF).reshape(steps, rows, out_cols)

    for copy in x_copies + rk_copies + b2_copies + dl_copies:
        copy.wait_send()
    for ky in range(n_y):
        b1_copies[ky].wait_send()


def shards(
    n_inst, n_tp,
    queries, stored_keys, stored_values, incoming_keys, incoming_values, cache_length_rows,
    output_matrix, adapter_down_weight, adapter_up_weight, host, slot,
):
    steps, rows, width = queries.shape
    adapters, _, rank = adapter_down_weight.shape
    out_cols = adapter_up_weight.shape[2]
    cap = max(1, 2 * rows // n_inst)
    pack = -(-steps * cap // TILE) * TILE
    total = n_inst * pack
    n_y = n_tp // 2
    lines = steps * rows
    operands = (
        host.reshape(1, rows), slot.reshape(1, rows), queries, incoming_keys,
        cache_length_rows.reshape(1, rows), stored_keys, incoming_values, stored_values,
        output_matrix, jnp.swapaxes(adapter_down_weight, 1, 2), adapter_up_weight,
    )
    vmem = pl.BlockSpec(memory_space=pltpu.VMEM)
    far = pl.BlockSpec(memory_space=pltpu.HBM)
    sem = pltpu.SemaphoreType.DMA
    return pl.pallas_call(
        functools.partial(kernel, n_inst, n_tp, cap),
        out_shape=pltpu.VMEM((steps, rows, out_cols), BF),
        in_specs=[far] * len(operands),
        out_specs=vmem,
        scratch_shapes=[
            *[pltpu.VMEM(operand.shape, operand.dtype) for operand in operands],
            pltpu.VMEM((n_inst, pack, width + LANES), BF),
            pltpu.VMEM((n_inst, pack, width + LANES), BF),
            pltpu.VMEM((n_inst, pack, out_cols), BF),
            pltpu.VMEM((n_inst, pack, out_cols), BF),
            pltpu.VMEM((total // 2, LANES), BF),
            pltpu.VMEM((n_tp, total // 2, LANES), BF),
            pltpu.VMEM((n_y, lines, out_cols), BF),
            pltpu.VMEM((n_y, lines, out_cols), BF),
            pltpu.VMEM((n_y, lines, out_cols), BF),
            pltpu.VMEM((n_y, lines, out_cols), BF),
            pltpu.VMEM((n_y, lines, out_cols), F32),
            sem((len(operands),)),
            sem((n_inst,)), sem((n_inst,)),
            sem((n_inst,)), sem((n_inst,)),
            sem((n_tp,)), sem((n_tp,)),
            sem((n_y,)), sem((n_y,)),
            sem((n_y,)), sem((n_y,)),
        ],
        compiler_params=pltpu.CompilerParams(
            collective_id=0, has_side_effects=True, vmem_limit_bytes=60 * 1024 * 1024
        ),
    )(*operands)


def solution(mesh):
    return jax.shard_map(
        functools.partial(shards, mesh.shape["inst"], mesh.shape["tp"]),
        mesh=mesh,
        in_specs=(
            P(None, "inst", "tp"),
            P("inst", None, "tp"),
            P("inst", None, "tp"),
            P(None, "inst", "tp"),
            P(None, "inst", "tp"),
            P("inst"),
            P("tp", None),
            P("inst", "tp", None),
            P("inst", None, "tp"),
            P("inst", None),
            P("inst"),
        ),
        out_specs=P(None, "inst", "tp"),
        check_vma=False,
    )
```

```python
import functools
import math

import jax
import jax.numpy as jnp
from jax import lax
from jax.experimental import pallas as pl
from jax.experimental.pallas import tpu as pltpu
from jax.sharding import PartitionSpec as P

MESH = pl.DeviceIdType.MESH
BF = jnp.bfloat16
F32 = jnp.float32
TILE = 16
LANES = 128
PIECES = 4


def log2(n):
    assert n & (n - 1) == 0
    return n.bit_length() - 1


def rows_iota(shape):
    return lax.broadcasted_iota(jnp.int32, shape, 0)


def lanes_iota(shape):
    return lax.broadcasted_iota(jnp.int32, shape, 1)


def dot(a, b):
    return jnp.dot(a, b, preferred_element_type=F32)


def dot_t(a, b):
    return lax.dot_general(a, b, (((1,), (1,)), ((), ())), preferred_element_type=F32)


def one_hot(mask):
    return jnp.where(mask, 1.0, 0.0).astype(BF)


def kernel(
    n_inst, n_tp, cap,
    host_hbm, slot_hbm, q_hbm, kn_hbm, len_hbm, k_hbm, vn_hbm, v_hbm, w_hbm, dn_hbm, up_hbm,
    out_ref,
    host_ref, slot_ref, q_ref, kn_ref, len_ref, k_buf, vn_ref, v_buf, w_buf, dn_buf, up_buf,
    x_s, x_r, dl_s, dl_r, rk_s, rk_r,
    b1_s, b1_r, b2_s, b2_r, own,
    in_sem, x_ss, x_rs, dl_ss, dl_rs, rk_ss, rk_rs,
    b1_ss, b1_rs, b2_ss, b2_rs,
):
    steps, rows, width = q_ref.shape
    head = kn_ref.shape[2]
    heads = width // head
    slots = k_buf.shape[1]
    per_row = steps * heads
    cols = rows * per_row
    pack = x_s.shape[1]
    total = n_inst * pack
    adapters, rank, _ = dn_buf.shape
    assert 2 * rank == LANES
    chunks = adapters * rank // LANES
    out_cols = up_buf.shape[2]
    n_y = n_tp // 2
    me = lax.axis_index("inst")
    tp = lax.axis_index("tp")
    y = tp // 2
    core = lax.rem(tp, 2)

    def inst_at(k):
        return (lax.rem(me + k + n_inst, n_inst), tp)

    def tp_at(k):
        return (me, lax.rem(tp + k, n_tp))

    def remote(src, dst, send, recv, where):
        return pltpu.make_async_remote_copy(
            src_ref=src, dst_ref=dst, send_sem=send, recv_sem=recv,
            device_id=where, device_id_type=MESH,
        )

    far_first = sorted(range(1, n_inst), key=lambda k: -min(k, n_inst - k))
    loads = []
    for at, (src, dst) in enumerate((
        (host_hbm, host_ref), (slot_hbm, slot_ref), (q_hbm, q_ref), (kn_hbm, kn_ref),
        (len_hbm, len_ref), (k_hbm, k_buf), (vn_hbm, vn_ref), (v_hbm, v_buf),
        (w_hbm, w_buf), (dn_hbm, dn_buf), (up_hbm, up_buf),
    )):
        load = pltpu.make_async_copy(src, dst, in_sem.at[at])
        if at < 8 and at not in (5, 7):
            load.start()
        loads.append(load)
    piece = rows // PIECES
    key_loads, value_loads = [], []
    for src, dst, kept, first in (
        (k_hbm, k_buf, key_loads, 11), (v_hbm, v_buf, value_loads, 11 + PIECES)
    ):
        for c in range(PIECES):
            at = pl.ds(c * piece, piece)
            load = pltpu.make_async_copy(src.at[at], dst.at[at], in_sem.at[first + c])
            load.start()
            kept.append(load)
    barrier = pltpu.get_barrier_semaphore()
    for k in range(1, n_inst):
        pl.semaphore_signal(barrier, inc=1, device_id=inst_at(k), device_id_type=MESH)
    for k in range(1, n_tp):
        pl.semaphore_signal(barrier, inc=1, device_id=tp_at(k), device_id_type=MESH)

    loads[0].wait()
    loads[1].wait()
    host_lane = host_ref[...].astype(F32)
    slot_lane = slot_ref[...].astype(F32)
    here = me.astype(F32)
    square = (rows, rows)
    ri, li = rows_iota(square), lanes_iota(square)
    host_col = jnp.sum(jnp.where(ri == li, host_lane, 0.0), axis=1, keepdims=True)
    same = jnp.broadcast_to(host_col, square) == jnp.broadcast_to(host_lane, square)
    pos_lane = jnp.sum(jnp.where(same & (ri < li), 1.0, 0.0), axis=0, keepdims=True)
    pos_col = jnp.sum(jnp.where(same & (li < ri), 1.0, 0.0), axis=1, keepdims=True)

    def place(host, pos):
        away = host - here
        away = jnp.where(away < 0.0, away + float(n_inst), away)
        return away * float(pack) + pos

    to_lane = place(host_lane, pos_lane).astype(jnp.int32)
    to_col = place(host_col, pos_col).astype(jnp.int32)
    pack_i = rows_iota((total, rows))
    packs = [pack_i == to_lane + step * cap for step in range(steps)]
    slot_packed = jnp.zeros((total, 1), F32)
    for chosen in packs:
        slot_packed += jnp.sum(jnp.where(chosen, slot_lane, 0.0), axis=1, keepdims=True)
    slot_packed = jnp.broadcast_to(slot_packed, (total, LANES)).astype(BF)
    x_s[:, :, width:] = slot_packed.reshape(n_inst, pack, LANES)
    x_r[0, :, width:] = slot_packed[:pack]

    ci = rows_iota((cols, cols))
    cj = lanes_iota((cols, cols))
    into = one_hot(cj == ((ci & (per_row - 1)) << log2(rows)) + (ci >> log2(per_row)))
    back = one_hot(ci == ((cj & (per_row - 1)) << log2(rows)) + (cj >> log2(per_row)))
    for load in loads[2:5]:
        load.wait()
    q_all = jnp.concatenate(
        [q_ref[s, :, h * head:(h + 1) * head] for s in range(steps) for h in range(heads)], axis=0
    )
    q_lines = dot(into, q_all)
    q_bf = q_lines.astype(BF)
    spread = rows_iota((cols, rows)) >> log2(per_row) == lanes_iota((cols, rows))
    lengths = jnp.sum(
        jnp.where(spread, len_ref[...].astype(F32), 0.0), axis=1, keepdims=True
    ).astype(jnp.int32)
    spread_bf = one_hot(spread)
    scale = 1.0 / math.sqrt(head)
    step_of = (rows_iota((cols, 1)) & (per_row - 1)) >> log2(heads)
    fresh = []
    for s in range(steps):
        value = jnp.sum(q_lines * dot(spread_bf, kn_ref[s]), axis=1, keepdims=True) * scale
        fresh.append(jnp.where(step_of >= s, value, -1e30))
    group = TILE // per_row
    group_of = rows_iota((TILE, slots)) >> log2(per_row)
    per_piece = piece // group
    for load in loads[8:]:
        load.start()
    scores = []
    for g in range(rows // group):
        if g % per_piece == 0:
            key_loads[g // per_piece].wait()
        keys = k_buf[g * group:(g + 1) * group].reshape(group * slots, head)
        raw = dot_t(q_bf[g * TILE:(g + 1) * TILE], keys)
        picked = raw[:, :slots]
        for j in range(1, group):
            picked = jnp.where(group_of == j, raw[:, j * slots:(j + 1) * slots], picked)
        scores.append(picked)
    scores = jnp.concatenate(scores, axis=0) * scale
    scores = jnp.where(lanes_iota((cols, slots)) < lengths, scores, -1e30)
    highest = jnp.max(scores, axis=1, keepdims=True)
    for value in fresh:
        highest = jnp.maximum(highest, value)
    cached_exp = jnp.exp(scores - highest)
    fresh_exp = [jnp.exp(value - highest) for value in fresh]
    denominator = jnp.sum(cached_exp, axis=1, keepdims=True)
    for value in fresh_exp:
        denominator += value
    weights = cached_exp / denominator
    mixed = jnp.zeros((cols, head), F32)
    loads[6].wait()
    for s in range(steps):
        share = (fresh_exp[s] / denominator).astype(BF).astype(F32)
        mixed += share * dot(spread_bf, vn_ref[s])
    parts = []
    for g in range(rows // group):
        if g % per_piece == 0:
            value_loads[g // per_piece].wait()
        values = v_buf[g * group:(g + 1) * group].reshape(group * slots, head)
        own_w = weights[g * TILE:(g + 1) * TILE]
        blocked = jnp.concatenate(
            [jnp.where(group_of == j, own_w, 0.0) for j in range(group)], axis=1
        ).astype(BF)
        parts.append(dot(blocked, values))
    mixed = (mixed + jnp.concatenate(parts, axis=0)).astype(BF)
    lines = dot(back, mixed).astype(BF)
    features = []
    for s in range(steps):
        at = s * heads * rows
        features.append(jnp.concatenate(
            [lines[at + h * rows:at + (h + 1) * rows] for h in range(heads)], axis=1
        ))

    packed = dot(one_hot(packs[0]), features[0])
    for s in range(1, steps):
        packed += dot(one_hot(packs[s]), features[s])
    packed = packed.astype(BF)
    x_s[:, :, :width] = packed.reshape(n_inst, pack, width)
    pl.semaphore_wait(barrier, n_inst - 1 + n_tp - 1)
    x_copies = []
    for k in far_first:
        copy = remote(x_s.at[k], x_r.at[k], x_ss.at[k], x_rs.at[k], inst_at(k))
        copy.start()
        x_copies.append(copy)
    x_r[0, :, :width] = packed[:pack]

    feats = jnp.concatenate(features, axis=0)
    loads[8].wait()

    def base_part(ky, parity):
        at = (lax.rem(y + ky, n_y) * 2 + parity) * out_cols
        return dot(feats, w_buf[:, pl.ds(pl.multiple_of(at, out_cols), out_cols)])

    b1_copies = {}
    for ky in reversed(range(n_y)):
        b1_s[ky] = base_part(ky, 1 - core).astype(BF)
        copy = remote(
            b1_s.at[ky], b1_r.at[ky], b1_ss.at[ky], b1_rs.at[ky], (me, y * 2 + 1 - core)
        )
        copy.start()
        b1_copies[ky] = copy
    loads[9].wait()
    for copy in x_copies:
        copy.wait_recv()
    slot_got = x_r[:, :, width:].reshape(total, LANES).astype(F32)
    lane = lanes_iota((total, LANES))
    masks = [
        slot_got == ((lane + c * LANES) >> log2(rank)).astype(F32) for c in range(chunks)
    ]
    ranked = dot_t(
        x_r[:, :, :width].reshape(total, width), dn_buf[...].reshape(adapters * rank, width)
    )
    folded = jnp.zeros((total, LANES), F32)
    for c in range(chunks):
        folded += jnp.where(masks[c], ranked[:, c * LANES:(c + 1) * LANES], 0.0)
    half = total // 2
    left = lanes_iota((half, LANES)) < rank
    both = folded + pltpu.roll(folded, LANES - rank, 1)
    paired = jnp.where(left, both[:half], both[half:])
    rk_s[...] = paired.astype(BF)
    rk_copies = []
    for k in range(1, n_tp):
        copy = remote(rk_s, rk_r.at[k], rk_ss.at[k], rk_rs.at[k], tp_at(k))
        copy.start()
        rk_copies.append(copy)

    for ky in reversed(range(n_y)):
        own[ky] = base_part(ky, core)
    b2_copies = []
    for ky in range(1, n_y):
        b1_copies[ky].wait_recv()
        b2_s[ky] = (own[ky] + b1_r[ky].astype(F32)).astype(BF)
        copy = remote(
            b2_s.at[ky], b2_r.at[ky], b2_ss.at[ky], b2_rs.at[ky],
            (me, lax.rem(y + ky, n_y) * 2 + core),
        )
        copy.start()
        b2_copies.append(copy)

    loads[10].wait()
    for k, copy in enumerate(rk_copies, 1):
        copy.wait_recv()
        paired += rk_r[k].astype(F32)
    turned = pltpu.roll(paired, LANES - rank, 1)
    folded = jnp.concatenate(
        [jnp.where(left, paired, turned), jnp.where(left, turned, paired)], axis=0
    )
    wide = jnp.concatenate(
        [jnp.where(masks[c], folded, 0.0) for c in range(chunks)], axis=1
    ).astype(BF)
    delta = dot(wide, up_buf[...].reshape(adapters * rank, out_cols)).astype(BF)
    dl_s[...] = delta.reshape(n_inst, pack, out_cols)
    dl_copies = []
    for k in far_first:
        copy = remote(dl_s.at[k], dl_r.at[k], dl_ss.at[k], dl_rs.at[k], inst_at(-k))
        copy.start()
        dl_copies.append(copy)
    dl_r[0] = delta[:pack]

    b1_copies[0].wait_recv()
    base = own[0] + b1_r[0].astype(F32)
    for ky, copy in enumerate(b2_copies, 1):
        copy.wait_recv()
        base += b2_r[ky].astype(F32)
    own[0] = base
    unpack = jnp.concatenate(
        [one_hot(lanes_iota((rows, total)) == to_col + step * cap) for step in range(steps)], axis=0
    )
    for copy in dl_copies:
        copy.wait_recv()
    result = own[0] + dot(unpack, dl_r[...].reshape(total, out_cols))
    out_ref[...] = result.astype(BF).reshape(steps, rows, out_cols)

    for copy in x_copies + rk_copies + b2_copies + dl_copies:
        copy.wait_send()
    for ky in range(n_y):
        b1_copies[ky].wait_send()


def shards(
    n_inst, n_tp,
    queries, stored_keys, stored_values, incoming_keys, incoming_values, cache_length_rows,
    output_matrix, adapter_down_weight, adapter_up_weight, host, slot,
):
    steps, rows, width = queries.shape
    adapters, _, rank = adapter_down_weight.shape
    out_cols = adapter_up_weight.shape[2]
    cap = max(1, 2 * rows // n_inst)
    pack = -(-steps * cap // TILE) * TILE
    total = n_inst * pack
    n_y = n_tp // 2
    lines = steps * rows
    operands = (
        host.reshape(1, rows), slot.reshape(1, rows), queries, incoming_keys,
        cache_length_rows.reshape(1, rows), stored_keys, incoming_values, stored_values,
        output_matrix, jnp.swapaxes(adapter_down_weight, 1, 2), adapter_up_weight,
    )
    vmem = pl.BlockSpec(memory_space=pltpu.VMEM)
    far = pl.BlockSpec(memory_space=pltpu.HBM)
    sem = pltpu.SemaphoreType.DMA
    return pl.pallas_call(
        functools.partial(kernel, n_inst, n_tp, cap),
        out_shape=pltpu.VMEM((steps, rows, out_cols), BF),
        in_specs=[far] * len(operands),
        out_specs=vmem,
        scratch_shapes=[
            *[pltpu.VMEM(operand.shape, operand.dtype) for operand in operands],
            pltpu.VMEM((n_inst, pack, width + LANES), BF),
            pltpu.VMEM((n_inst, pack, width + LANES), BF),
            pltpu.VMEM((n_inst, pack, out_cols), BF),
            pltpu.VMEM((n_inst, pack, out_cols), BF),
            pltpu.VMEM((total // 2, LANES), BF),
            pltpu.VMEM((n_tp, total // 2, LANES), BF),
            pltpu.VMEM((n_y, lines, out_cols), BF),
            pltpu.VMEM((n_y, lines, out_cols), BF),
            pltpu.VMEM((n_y, lines, out_cols), BF),
            pltpu.VMEM((n_y, lines, out_cols), BF),
            pltpu.VMEM((n_y, lines, out_cols), F32),
            sem((len(operands) + 2 * PIECES,)),
            sem((n_inst,)), sem((n_inst,)),
            sem((n_inst,)), sem((n_inst,)),
            sem((n_tp,)), sem((n_tp,)),
            sem((n_y,)), sem((n_y,)),
            sem((n_y,)), sem((n_y,)),
        ],
        compiler_params=pltpu.CompilerParams(
            collective_id=0, has_side_effects=True, vmem_limit_bytes=60 * 1024 * 1024
        ),
    )(*operands)


def solution(mesh):
    return jax.shard_map(
        functools.partial(shards, mesh.shape["inst"], mesh.shape["tp"]),
        mesh=mesh,
        in_specs=(
            P(None, "inst", "tp"),
            P("inst", None, "tp"),
            P("inst", None, "tp"),
            P(None, "inst", "tp"),
            P(None, "inst", "tp"),
            P("inst"),
            P("tp", None),
            P("inst", "tp", None),
            P("inst", None, "tp"),
            P("inst", None),
            P("inst"),
        ),
        out_specs=P(None, "inst", "tp"),
        check_vma=False,
    )
```
